32 devices in a mesh: groups: 2 (over y), row: 2 (over x), col: 4 (over z), head: 2 (over core).
Axes of the slice: x: 2, y: 2, z: 4, core: 2. Of those that a mesh axis runs over, the one named last changes fastest.
Arguments:
- pair_rep: bfloat16 [96, 48, 128], P(('groups', 'col'), 'row'), parts along dimension 0, may hold values from -4.5 to 4.5
- pad_mask: int32 [96], P('groups'), parts along dimension 0, may hold values from 0 to 1, as said below
- chain_breaks: int32 [8], P('groups'), parts along dimension 0, may hold values from 1 to 47, as said below
- w_query: bfloat16 [128, 128], P(None, 'head'), may hold values from -0.5 to 0.5
- w_key: bfloat16 [128, 128], P(None, 'head'), may hold values from -0.5 to 0.5
- w_value: bfloat16 [128, 128], P(None, 'head'), may hold values from -0.5 to 0.5
- w_gate: bfloat16 [128, 128], P(None, 'head'), may hold values from -0.5 to 0.5
- w_bias: bfloat16 [128, 4], P(None, 'head'), may hold values from -8 to 8
- chain_bias: float32 [4], P('head'), may hold values from -2 to 2
- w_out: bfloat16 [128, 128], P('head'), may hold values from -6 to 6
Outputs:
- update: bfloat16 [96, 48, 128], P(('groups', 'col'), 'row', 'head'), parts along dimension 0
The draws below stay inside these ranges and needn't reach their ends.
There are 2 independent parts, one for each index of `groups`. The reference program is written for one: setup_inputs(seed, part) draws one part's arguments, and reference() takes and returns one part's arrays. A program takes and returns all parts, laid end to end along the dimension named above; an argument that names none is the same for every part. Nothing has to cross between parts.
Inputs may be any that keep to these rules, and one draw needn't show every extreme that they name: `pad_mask`: 1 on a prefix of 24 to 42 residues and 0 after it. `chain_breaks`: strictly increasing.
All inputs are finite; a program needn't handle non-finite values.
Results may differ from the reference program's by a relative error of at most 0.014.
Values may be sent and summed in bfloat16 or wider, within the bound.
A program may use at most 64 MiB of HBM per device.

```python
import math
import jax
import jax.numpy as jnp
from jax import lax

C = 128
HEADS = 4
HD = 32
NBREAK = 4
N = 48


def draw_pair_rep(key, part):
    drawn = jnp.clip(jax.random.normal(key, (N, N, C), jnp.float32), -4.5, 4.5)
    return drawn.astype(jnp.bfloat16)


def draw_pad_mask(key, part):
    lowest = N // 2
    span = 7 * N // 8 - lowest
    steps_drawn = jax.random.randint(key, (), 0, (span - 1) // 2 + 1)
    length = lowest + jnp.asarray(part, jnp.int32) % 2 + 2 * steps_drawn
    return (jnp.arange(N) < length).astype(jnp.int32)


def draw_chain_breaks(key, part):
    chosen = jax.random.permutation(key, N - 2)[:NBREAK - 1] + 1
    last_break = jnp.full((1,), N - 1, jnp.int32)
    return jnp.sort(jnp.concatenate([chosen.astype(jnp.int32), last_break])).astype(jnp.int32)


def draw_w_bias(key, part):
    noise_draw = jax.random.normal(key, (C, HEADS), jnp.float32)
    return (noise_draw / math.sqrt(C)).astype(jnp.bfloat16)


def shard_levels(key, dims, split, least, largest):
    gain, own = 1.0, jax.random.fold_in(key, 6)
    for position, blocks in split:
        steps = jnp.exp(jax.random.uniform(jax.random.fold_in(own, position), (blocks,), jnp.float32, least / len(split), largest / len(split)))
        gain = gain * jnp.repeat(steps, dims[position] // blocks).reshape([-1 if axis == position else 1 for axis in range(len(dims))])
    return gain


def bell_draw(rng, dims, width, bound, shards=(), held_as=jnp.bfloat16):
    entries = jax.random.normal(rng, dims, jnp.float32) * width
    if len(shards) > 0:
        entries = shard_levels(rng, dims, shards, -0.22, 0.18) * entries
    return jnp.clip(entries, min=-bound, max=bound).astype(held_as)


def setup_inputs(seed: int = 0, part: int = 0) -> dict:
    key_of = jax.random.split(jax.random.key(seed), 11)
    part_keys = jax.random.split(jax.random.fold_in(key_of[10], part), 11)
    pair_rep = draw_pair_rep(jax.random.fold_in(jax.random.fold_in(key_of[10], part), 71), part)
    pad_mask = draw_pad_mask(jax.random.fold_in(jax.random.fold_in(key_of[10], part), 71), part)
    chain_breaks = draw_chain_breaks(jax.random.fold_in(jax.random.fold_in(key_of[10], part), 71), part)
    w_query = bell_draw(key_of[3], (C, HEADS * HD), C ** -0.5, 0.5, ((1, 2),))
    w_key = bell_draw(key_of[4], (C, HEADS * HD), C ** -0.5, 0.5, ((1, 2),))
    w_value = bell_draw(key_of[5], (C, HEADS * HD), C ** -0.5, 0.5, ((1, 2),))
    w_gate = bell_draw(key_of[6], (C, HEADS * HD), C ** -0.5, 0.5, ((1, 2),))
    w_bias = draw_w_bias(jax.random.fold_in(key_of[10], 71), part)
    chain_bias = jnp.clip(jax.random.uniform(key_of[8], (HEADS,), jnp.float32, -2.0, 2.0) * shard_levels(key_of[8], (HEADS,), ((0, 2),), -0.4, 0.0), -2.0, 2.0)
    w_out = bell_draw(key_of[9], (HEADS * HD, C), 1.0, 6.0, ((0, 2),))
    return {"pair_rep": pair_rep, "pad_mask": pad_mask, "chain_breaks": chain_breaks, "w_query": w_query, "w_key": w_key, "w_value": w_value, "w_gate": w_gate, "w_bias": w_bias, "chain_bias": chain_bias, "w_out": w_out}


def layer_norm(pair_rep):
    as_float = pair_rep.astype(jnp.float32)
    centred = as_float - lax.optimization_barrier(jnp.mean(as_float, axis=-1, keepdims=True))
    spread = lax.optimization_barrier(jnp.mean(centred * centred, axis=-1, keepdims=True))
    return (centred * lax.rsqrt(spread + 1e-05)).astype(jnp.bfloat16)

def chain_number(positions, chain_breaks):
    return lax.optimization_barrier(jnp.sum((chain_breaks[None, :] <= positions[:, None]).astype(jnp.int32), axis=1))

def pair_terms(query_pos, key_pos, chain_breaks, key_flags, chain_bias):
    across_chain = (chain_number(query_pos, chain_breaks)[:, None] != chain_number(key_pos, chain_breaks)[None, :]).astype(jnp.float32)
    mask_term = (key_flags.astype(jnp.float32) - 1.0) * 1000000000.0
    return chain_bias.astype(jnp.float32)[:, None, None] * across_chain[None] + mask_term[None, None, :]

def reference(pair_rep, pad_mask, chain_breaks, w_query, w_key, w_value, w_gate, w_bias, chain_bias, w_out):
    normed = layer_norm(pair_rep)
    flat_rows = normed.reshape(N * N, C)
    queries = (jnp.dot(flat_rows, w_query, preferred_element_type=jnp.float32) * HD ** (-0.5)).astype(jnp.bfloat16).reshape(N, N, HEADS, HD)
    key_heads = jnp.dot(flat_rows, w_key, preferred_element_type=jnp.float32).astype(jnp.bfloat16).reshape(N, N, HEADS, HD)
    value_heads = jnp.dot(flat_rows, w_value, preferred_element_type=jnp.float32).astype(jnp.bfloat16).reshape(N, N, HEADS, HD)
    gating = jax.nn.sigmoid(jnp.dot(flat_rows, w_gate, preferred_element_type=jnp.float32)).astype(jnp.bfloat16)
    pair_bias = jnp.transpose(jnp.dot(flat_rows, w_bias, preferred_element_type=jnp.float32).reshape(N, N, HEADS), (2, 0, 1))
    positions = jnp.arange(N, dtype=jnp.int32)
    extra_all = pair_terms(positions, positions, chain_breaks, pad_mask, chain_bias)

    def one_row(pieces):
        q_row, k_row, v_row = pieces
        scores = jnp.einsum('jhd,khd->hjk', q_row.astype(jnp.float32), k_row.astype(jnp.float32))
        scores = scores + pair_bias
        scores = scores + extra_all
        row_max = lax.optimization_barrier(jnp.max(scores, axis=-1, keepdims=True))
        weights = jnp.exp(scores - row_max)
        row_sum = lax.optimization_barrier(jnp.sum(weights, axis=-1))
        rounded = lax.optimization_barrier(weights.astype(jnp.bfloat16)).astype(jnp.float32)
        mixed_rows = jnp.einsum('hjk,khd->jhd', rounded, v_row.astype(jnp.float32))
        return (mixed_rows / jnp.transpose(row_sum)[:, :, None]).astype(jnp.bfloat16)
    attended = lax.map(one_row, (queries, key_heads, value_heads))
    combined = (gating.astype(jnp.float32) * attended.reshape(N * N, HEADS * HD).astype(jnp.float32)).astype(jnp.bfloat16)
    return jnp.dot(combined, w_out, preferred_element_type=jnp.float32).astype(jnp.bfloat16).reshape(N, N, C)
```

```python
import functools

import jax
import jax.numpy as jnp
from jax import lax
from jax.experimental import pallas as pl
from jax.experimental.pallas import tpu as pltpu
from jax.sharding import PartitionSpec as P

HD = 32
MESH = pl.DeviceIdType.MESH
F32 = jnp.float32
BF16 = jnp.bfloat16
NT = (((1,), (1,)), ((), ()))


def layer_norm(x):
    centred = x - jnp.mean(x, axis=-1, keepdims=True)
    spread = jnp.mean(centred * centred, axis=-1, keepdims=True)
    return centred * lax.rsqrt(spread + 1e-05)


def dot(a, b):
    return jnp.dot(a, b, preferred_element_type=F32)


def largest_divisor(n, limit, step=1):
    best = step
    for d in range(step, n + 1, step):
        if n % d == 0 and d <= limit:
            best = d
    return best


def kernel(
    sizes,
    pair, mask, breaks, chain_bias, wq, wk, wv, wg, wb, wo,
    out,
    xs, wbuf, wbbuf, wobuf, qg, kv, bsend, brecv, bfull, gown, goth,
    local_sem, x_send, x_recv, wo_send, wo_recv, b_send, b_recv, g_send, g_recv,
):
    rows, cols, heads, n_i, n_j, n_h, channels = sizes
    n_k = rows * n_j
    hw = n_h * HD
    piece = bsend.shape[2]
    r, c, h = lax.axis_index("row"), lax.axis_index("col"), lax.axis_index("head")

    barrier = pltpu.get_barrier_semaphore()
    for r2 in range(rows):
        for c2 in range(cols):
            @pl.when(jnp.logical_or(r != r2, c != c2))
            def _():
                pl.semaphore_signal(
                    barrier, inc=1, device_id={"row": r2, "col": c2}, device_id_type=MESH
                )
    for d in range(1, heads):
        pl.semaphore_signal(
            barrier, inc=1, device_id={"head": lax.rem(h + d, heads)}, device_id_type=MESH
        )

    locals_ = [
        pltpu.make_async_copy(pair, xs.at[r], local_sem.at[0]),
        pltpu.make_async_copy(wb, wbbuf, local_sem.at[1]),
        pltpu.make_async_copy(wq, wbuf.at[0], local_sem.at[2]),
        pltpu.make_async_copy(wg, wbuf.at[1], local_sem.at[3]),
        pltpu.make_async_copy(wk, wbuf.at[2], local_sem.at[4]),
        pltpu.make_async_copy(wv, wbuf.at[3], local_sem.at[5]),
        pltpu.make_async_copy(wo, wobuf.at[0], local_sem.at[6]),
    ]
    for copy in locals_:
        copy.start()

    pl.semaphore_wait(barrier, rows * cols - 1 + heads - 1)

    x_copies = []
    for d in range(1, rows):
        copy = pltpu.make_async_remote_copy(
            src_ref=pair, dst_ref=xs.at[r], send_sem=x_send.at[d], recv_sem=x_recv.at[d],
            device_id={"row": lax.rem(r + d, rows)}, device_id_type=MESH,
        )
        copy.start()
        x_copies.append(copy)
    wo_copies = []
    for d in range(1, heads):
        copy = pltpu.make_async_remote_copy(
            src_ref=wo, dst_ref=wobuf.at[d], send_sem=wo_send.at[d], recv_sem=wo_recv.at[d],
            device_id={"head": lax.rem(h + d, heads)}, device_id_type=MESH,
        )
        copy.start()
        wo_copies.append(copy)

    for copy in locals_:
        copy.wait()

    wide = lambda a, b: jnp.concatenate(
        [wbuf[a].astype(F32), wbuf[b].astype(F32)], axis=1
    ).astype(BF16)
    wqg, wkv = wide(0, 1), wide(2, 3)
    wb_square = jnp.concatenate(
        [wbbuf[...].astype(F32), jnp.zeros((channels, channels - n_h), F32)], axis=1
    )
    wbt = wb_square.T[:16].astype(BF16)

    lane = lax.broadcasted_iota(jnp.int32, (1, 2 * hw), 1)
    step_i = largest_divisor(n_i, 12, 2)
    flat = step_i * n_j
    own_normed = []
    for first in range(0, n_i, step_i):
        normed = layer_norm(xs[r, pl.ds(first * n_j, flat), :].astype(F32))
        normed3 = normed.reshape(step_i, n_j, channels).astype(BF16)
        for i in range(step_i):
            line = lax.dot_general(wbt, normed3[i], NT, preferred_element_type=F32)
            p, at = divmod(first + i, piece)
            for head in range(n_h):
                bsend[p, head, pl.ds(at, 1), :] = line[head : head + 1]
        own_normed.append(normed.astype(BF16))

    def bias_copy(p, c2):
        start = c * n_i + p * piece
        target = start // n_j
        slot = (start - target * n_j) // piece
        return target, slot, pltpu.make_async_remote_copy(
            src_ref=bsend.at[p], dst_ref=brecv.at[r, slot],
            send_sem=b_send.at[p, c2], recv_sem=b_recv.at[r, slot],
            device_id={"row": target, "col": c2}, device_id_type=MESH,
        )

    pieces_sent = n_i // piece
    for p in range(pieces_sent):
        for c2 in range(cols):
            target, slot, copy = bias_copy(p, c2)
            here = jnp.logical_and(target == r, c == c2)

            @pl.when(jnp.logical_not(here))
            def _():
                copy.start()

            @pl.when(here)
            def _():
                brecv[r, slot] = bsend[p]

    for step, first in enumerate(range(0, n_i, step_i)):
        at = pl.ds(first * n_j, flat)
        both = dot(own_normed[step], wqg)
        qg[at, :] = jnp.where(
            lane < hw, (both * HD ** (-0.5)).astype(BF16).astype(F32),
            jax.nn.sigmoid(both).astype(BF16).astype(F32),
        )
        kv[r, at, :] = dot(own_normed[step], wkv)

    key_pos = lax.broadcasted_iota(jnp.int32, (n_j, n_k), 1)
    query_pos = r * n_j + lax.broadcasted_iota(jnp.int32, (n_j, n_k), 0)
    key_chain = jnp.zeros((n_j, n_k), jnp.int32)
    query_chain = jnp.zeros((n_j, n_k), jnp.int32)
    for b in range(breaks.shape[0]):
        key_chain += (breaks[b] <= key_pos).astype(jnp.int32)
        query_chain += (breaks[b] <= query_pos).astype(jnp.int32)
    across = (key_chain != query_chain).astype(F32)
    mask_term = (mask[...].astype(F32) - 1.0) * 1000000000.0

    own_rows = wobuf.shape[1]
    share = wobuf.shape[2] // heads

    def out_weight(d):
        full = wobuf[d].astype(F32)
        mine = full[:, :share]
        for t in range(1, heads):
            mine = jnp.where(h == t, full[:, t * share : (t + 1) * share], mine)
        return jnp.concatenate([jnp.zeros((hw, share), F32), mine], axis=0).astype(BF16)

    for copy in wo_copies:
        copy.wait()
    out_weights = [out_weight(d) for d in range(heads)]

    for d in range(1, rows):
        x_copies[d - 1].wait()
        source = lax.rem(r + rows - d, rows)
        for first in range(0, n_i, step_i):
            at = pl.ds(first * n_j, flat)
            normed = layer_norm(xs[source, at, :].astype(F32)).astype(BF16)
            kv[source, at, :] = dot(normed, wkv)

    slots = n_j // piece
    for slot in range(slots):
        source_c = (r * n_j + slot * piece) // n_i
        for r2 in range(rows):
            @pl.when(jnp.logical_or(r2 != r, source_c != c))
            def _():
                pltpu.make_async_remote_copy(
                    src_ref=bsend.at[0], dst_ref=brecv.at[r2, slot],
                    send_sem=b_send.at[0, 0], recv_sem=b_recv.at[r2, slot],
                    device_id={"row": r2}, device_id_type=MESH,
                ).wait_recv()
    for slot in range(slots):
        for r2 in range(rows):
            for head in range(n_h):
                bfull[head, pl.ds(slot * piece, piece), pl.ds(r2 * n_j, n_j)] = brecv[
                    r2, slot, head
                ]
    bias = jnp.concatenate(
        [bfull[head] + (chain_bias[head] * across + mask_term) for head in range(n_h)], axis=0
    )

    lanes_k = -(-n_k // 128) * 128
    step_a = largest_divisor(n_i, max(2, 40 * 1024 // (n_h * n_j * lanes_k)), 2)
    flat_a = step_a * n_j
    steps = n_i // step_a

    def gated_copy(step, d, at):
        return pltpu.make_async_remote_copy(
            src_ref=gown.at[at, :], dst_ref=goth.at[d, at, :],
            send_sem=g_send.at[d, step], recv_sem=g_recv.at[d, step],
            device_id={"head": lax.rem(h + d, heads)}, device_id_type=MESH,
        )

    def attend(step):
        at = pl.ds(pl.multiple_of(step * flat_a, 16), flat_a)
        qg3 = qg[at, :].reshape(step_a, n_j, 2 * hw)
        queries = jnp.concatenate(
            [
                jnp.where(jnp.logical_and(lane >= t * HD, lane < (t + 1) * HD)[None], qg3, 0.0)
                for t in range(n_h)
            ],
            axis=1,
        ).astype(BF16)
        keys = jnp.concatenate(
            [kv[r2, at, :].reshape(step_a, n_j, 2 * hw) for r2 in range(rows)], axis=1
        ).astype(BF16)
        scores = lax.dot_general(
            queries, keys, (((2,), (2,)), ((0,), (0,))), preferred_element_type=F32
        ) + bias[None]
        weights = jnp.exp(scores - jnp.max(scores, axis=-1, keepdims=True))
        total = jnp.sum(weights, axis=-1, keepdims=True)
        mixed = lax.dot_general(
            weights.astype(BF16), keys, (((2,), (1,)), ((0,), (0,))), preferred_element_type=F32
        ) / total
        attended = mixed[:, :n_j]
        for t in range(1, n_h):
            attended = jnp.where(
                (lane >= hw + t * HD)[None], mixed[:, t * n_j : (t + 1) * n_j], attended
            )
        gated = jnp.where(
            (lane >= hw)[None], attended.astype(BF16).astype(F32) * qg3, 0.0
        )
        gown[at, :] = gated.reshape(flat_a, 2 * hw).astype(BF16)
        for d in range(1, heads):
            gated_copy(step, d, at).start()

    def project(step):
        at = pl.ds(pl.multiple_of(step * flat_a, 16), flat_a)
        acc = dot(gown[at, :], out_weights[0])
        for d in range(1, heads):
            gated_copy(step, d, at).wait()
            acc += dot(goth[d, at, :], out_weights[d])
        out[at, :] = acc.astype(out.dtype)

    if steps <= 4:
        for step in range(steps):
            attend(step)
        for step in range(steps):
            project(step)
    else:
        pl.loop(0, steps)(attend)
        pl.loop(0, steps)(project)

    for p in range(pieces_sent):
        for c2 in range(cols):
            target, slot, copy = bias_copy(p, c2)

            @pl.when(jnp.logical_or(target != r, c != c2))
            def _():
                copy.wait_send()


def per_device(
    mesh_sizes, pair_rep, pad_mask, chain_breaks, w_query, w_key, w_value, w_gate, w_bias,
    chain_bias, w_out
):
    rows, cols, heads = mesh_sizes
    n_i, n_j, channels = pair_rep.shape
    n_h = chain_bias.shape[0]
    hw = n_h * HD
    n_k = rows * n_j
    total = n_i * n_j
    piece = min(n_i, n_j)
    lanes_k = -(-n_k // 128) * 128
    step_a = largest_divisor(n_i, max(2, 40 * 1024 // (n_h * n_j * lanes_k)), 2)
    steps = n_i // step_a
    share = w_out.shape[1] // heads
    any_spec = pl.BlockSpec(memory_space=pl.ANY)
    smem = pl.BlockSpec(memory_space=pltpu.SMEM)
    vmem = pl.BlockSpec(memory_space=pltpu.VMEM)
    dma = pltpu.SemaphoreType.DMA
    scratch = [
        pltpu.VMEM((rows, total, channels), BF16),
        pltpu.VMEM((4, channels, hw), BF16),
        pltpu.VMEM((channels, n_h), BF16),
        pltpu.VMEM((heads, hw, w_out.shape[1]), BF16),
        pltpu.VMEM((total, 2 * hw), F32),
        pltpu.VMEM((rows, total, 2 * hw), F32),
        pltpu.VMEM((n_i // piece, n_h, piece, n_j), F32),
        pltpu.VMEM((rows, n_j // piece, n_h, piece, n_j), F32),
        pltpu.VMEM((n_h, n_j, n_k), F32),
        pltpu.VMEM((total, 2 * hw), BF16),
        pltpu.VMEM((heads, total, 2 * hw), BF16),
        dma((7,)),
        dma((rows,)),
        dma((rows,)),
        dma((heads,)),
        dma((heads,)),
        dma((n_i // piece, cols)),
        dma((rows, n_j // piece)),
        dma((heads, steps)),
        dma((heads, steps)),
    ]
    held = rows * total * 128 * 6 + total * 128 * 12
    update = pl.pallas_call(
        functools.partial(kernel, (rows, cols, heads, n_i, n_j, n_h, channels)),
        out_shape=jax.ShapeDtypeStruct((total, share), BF16),
        in_specs=[any_spec, vmem, smem, smem] + [any_spec] * 6,
        out_specs=vmem,
        scratch_shapes=scratch,
        compiler_params=pltpu.CompilerParams(
            collective_id=0,
            has_side_effects=True,
            vmem_limit_bytes=min(60 << 20, 2 * held + (8 << 20)),
        ),
    )(
        pair_rep.reshape(total, channels), pad_mask.reshape(1, n_k), chain_breaks, chain_bias,
        w_query, w_key, w_value, w_gate, w_bias, w_out,
    )
    return update.reshape(n_i, n_j, share)


def solution(mesh):
    placed = (
        P(("groups", "col"), "row", None),
        P("groups"),
        P("groups"),
        P(None, "head"),
        P(None, "head"),
        P(None, "head"),
        P(None, "head"),
        P(None, "head"),
        P("head"),
        P("head", None),
    )
    sizes = (mesh.shape["row"], mesh.shape["col"], mesh.shape["head"])
    return jax.shard_map(
        functools.partial(per_device, sizes),
        mesh=mesh,
        in_specs=placed,
        out_specs=P(("groups", "col"), "row", "head"),
        check_vma=False,
    )
```

```python
import functools

import jax
import jax.numpy as jnp
from jax import lax
from jax.experimental import pallas as pl
from jax.experimental.pallas import tpu as pltpu
from jax.sharding import PartitionSpec as P

HD = 32
MESH = pl.DeviceIdType.MESH
F32 = jnp.float32
BF16 = jnp.bfloat16
NT = (((1,), (1,)), ((), ()))


def layer_norm(x):
    centred = x - jnp.mean(x, axis=-1, keepdims=True)
    spread = jnp.mean(centred * centred, axis=-1, keepdims=True)
    return centred * lax.rsqrt(spread + 1e-05)


def dot(a, b):
    return jnp.dot(a, b, preferred_element_type=F32)


def dot_t(a, b):
    return lax.dot_general(a, b, NT, preferred_element_type=F32)


def largest_divisor(n, limit, step=1):
    best = step
    for d in range(step, n + 1, step):
        if n % d == 0 and d <= limit:
            best = d
    return best


def kernel(
    sizes,
    pair, mask, breaks, chain_bias, wq, wk, wv, wg, wb, wo,
    out,
    xs, wbuf, wbbuf, wobuf, maskbuf, breakbuf, cbbuf, qg, kv, bsend, brecv, bfull, gown, goth,
    local_sem, x_send, x_recv, wo_send, wo_recv, b_send, b_recv, g_send, g_recv,
):
    rows, cols, heads, n_i, n_j, n_h, channels = sizes
    n_k = rows * n_j
    hw = n_h * HD
    piece = bsend.shape[2]
    r, c, h = lax.axis_index("row"), lax.axis_index("col"), lax.axis_index("head")

    barrier = pltpu.get_barrier_semaphore()
    for r2 in range(rows):
        for c2 in range(cols):
            @pl.when(jnp.logical_or(r != r2, c != c2))
            def _():
                pl.semaphore_signal(
                    barrier, inc=1, device_id={"row": r2, "col": c2}, device_id_type=MESH
                )
    for d in range(1, heads):
        pl.semaphore_signal(
            barrier, inc=1, device_id={"head": lax.rem(h + d, heads)}, device_id_type=MESH
        )

    locals_ = [
        pltpu.make_async_copy(pair, xs.at[r], local_sem.at[0]),
        pltpu.make_async_copy(wb, wbbuf, local_sem.at[1]),
        pltpu.make_async_copy(wq, wbuf.at[0, pl.ds(0, hw)], local_sem.at[2]),
        pltpu.make_async_copy(wg, wbuf.at[0, pl.ds(hw, hw)], local_sem.at[3]),
        pltpu.make_async_copy(wk, wbuf.at[1, pl.ds(0, hw)], local_sem.at[4]),
        pltpu.make_async_copy(wv, wbuf.at[1, pl.ds(hw, hw)], local_sem.at[5]),
        pltpu.make_async_copy(wo, wobuf.at[0], local_sem.at[6]),
        pltpu.make_async_copy(mask, maskbuf, local_sem.at[7]),
        pltpu.make_async_copy(breaks, breakbuf, local_sem.at[8]),
        pltpu.make_async_copy(chain_bias, cbbuf, local_sem.at[9]),
    ]
    for copy in locals_:
        copy.start()

    pl.semaphore_wait(barrier, rows * cols - 1 + heads - 1)

    x_copies = []
    for d in range(1, rows):
        copy = pltpu.make_async_remote_copy(
            src_ref=pair, dst_ref=xs.at[r], send_sem=x_send.at[d], recv_sem=x_recv.at[d],
            device_id={"row": lax.rem(r + d, rows)}, device_id_type=MESH,
        )
        copy.start()
        x_copies.append(copy)
    wo_copies = []
    for d in range(1, heads):
        copy = pltpu.make_async_remote_copy(
            src_ref=wo, dst_ref=wobuf.at[d], send_sem=wo_send.at[d], recv_sem=wo_recv.at[d],
            device_id={"head": lax.rem(h + d, heads)}, device_id_type=MESH,
        )
        copy.start()
        wo_copies.append(copy)

    for copy in locals_:
        copy.wait()

    wqg, wkv = wbuf[0], wbuf[1]
    wbt = jnp.concatenate(
        [wbbuf[...].astype(F32), jnp.zeros((16 - n_h, channels), F32)], axis=0
    ).astype(BF16)

    lane = lax.broadcasted_iota(jnp.int32, (1, 2 * hw), 1)
    step_i = largest_divisor(n_i, 12, 2)
    flat = step_i * n_j
    own_normed = []
    for first in range(0, n_i, step_i):
        normed = layer_norm(xs[r, pl.ds(first * n_j, flat), :].astype(F32))
        normed3 = normed.reshape(step_i, n_j, channels).astype(BF16)
        for i in range(step_i):
            line = lax.dot_general(wbt, normed3[i], NT, preferred_element_type=F32)
            p, at = divmod(first + i, piece)
            for head in range(n_h):
                bsend[p, head, pl.ds(at, 1), :] = line[head : head + 1]
        own_normed.append(normed.astype(BF16))

    def bias_copy(p, c2):
        start = c * n_i + p * piece
        target = start // n_j
        slot = (start - target * n_j) // piece
        return target, slot, pltpu.make_async_remote_copy(
            src_ref=bsend.at[p], dst_ref=brecv.at[r, slot],
            send_sem=b_send.at[p, c2], recv_sem=b_recv.at[r, slot],
            device_id={"row": target, "col": c2}, device_id_type=MESH,
        )

    pieces_sent = n_i // piece
    for p in range(pieces_sent):
        for c2 in range(cols):
            target, slot, copy = bias_copy(p, c2)
            here = jnp.logical_and(target == r, c == c2)

            @pl.when(jnp.logical_not(here))
            def _():
                copy.start()

            @pl.when(here)
            def _():
                brecv[r, slot] = bsend[p]

    for step, first in enumerate(range(0, n_i, step_i)):
        at = pl.ds(first * n_j, flat)
        both = dot_t(own_normed[step], wqg)
        qg[at, :] = jnp.where(
            lane < hw, (both * HD ** (-0.5)).astype(BF16).astype(F32),
            jax.nn.sigmoid(both).astype(BF16).astype(F32),
        )
        kv[r, at, :] = dot_t(own_normed[step], wkv)

    key_pos = lax.broadcasted_iota(jnp.int32, (n_j, n_k), 1)
    query_pos = r * n_j + lax.broadcasted_iota(jnp.int32, (n_j, n_k), 0)
    key_chain = jnp.zeros((n_j, n_k), jnp.int32)
    query_chain = jnp.zeros((n_j, n_k), jnp.int32)
    for b in range(breaks.shape[0]):
        key_chain += (breakbuf[b] <= key_pos).astype(jnp.int32)
        query_chain += (breakbuf[b] <= query_pos).astype(jnp.int32)
    across = (key_chain != query_chain).astype(F32)
    mask_term = (maskbuf[...].astype(F32) - 1.0) * 1000000000.0

    own_rows = wobuf.shape[1]
    share = wobuf.shape[2] // heads

    def out_weight(d):
        full = wobuf[d].astype(F32)
        mine = full[:, :share]
        for t in range(1, heads):
            mine = jnp.where(h == t, full[:, t * share : (t + 1) * share], mine)
        return jnp.concatenate([jnp.zeros((hw, share), F32), mine], axis=0).astype(BF16)

    for copy in wo_copies:
        copy.wait()
    out_weights = [out_weight(d) for d in range(heads)]

    for d in range(1, rows):
        x_copies[d - 1].wait()
        source = lax.rem(r + rows - d, rows)
        for first in range(0, n_i, step_i):
            at = pl.ds(first * n_j, flat)
            normed = layer_norm(xs[source, at, :].astype(F32)).astype(BF16)
            kv[source, at, :] = dot_t(normed, wkv)

    slots = n_j // piece
    for slot in range(slots):
        source_c = (r * n_j + slot * piece) // n_i
        for r2 in range(rows):
            @pl.when(jnp.logical_or(r2 != r, source_c != c))
            def _():
                pltpu.make_async_remote_copy(
                    src_ref=bsend.at[0], dst_ref=brecv.at[r2, slot],
                    send_sem=b_send.at[0, 0], recv_sem=b_recv.at[r2, slot],
                    device_id={"row": r2}, device_id_type=MESH,
                ).wait_recv()
    for slot in range(slots):
        for r2 in range(rows):
            for head in range(n_h):
                bfull[head, pl.ds(slot * piece, piece), pl.ds(r2 * n_j, n_j)] = brecv[
                    r2, slot, head
                ]
    bias = jnp.concatenate(
        [bfull[head] + (cbbuf[head] * across + mask_term) for head in range(n_h)], axis=0
    )

    lanes_k = -(-n_k // 128) * 128
    step_a = largest_divisor(n_i, max(2, 40 * 1024 // (n_h * n_j * lanes_k)), 2)
    flat_a = step_a * n_j
    steps = n_i // step_a

    def gated_copy(step, d, at):
        return pltpu.make_async_remote_copy(
            src_ref=gown.at[at, :], dst_ref=goth.at[d, at, :],
            send_sem=g_send.at[d, step], recv_sem=g_recv.at[d, step],
            device_id={"head": lax.rem(h + d, heads)}, device_id_type=MESH,
        )

    def attend(step):
        at = pl.ds(pl.multiple_of(step * flat_a, 16), flat_a)
        qg3 = qg[at, :].reshape(step_a, n_j, 2 * hw)
        queries = jnp.concatenate(
            [
                jnp.where(jnp.logical_and(lane >= t * HD, lane < (t + 1) * HD)[None], qg3, 0.0)
                for t in range(n_h)
            ],
            axis=1,
        ).astype(BF16)
        keys = jnp.concatenate(
            [kv[r2, at, :].reshape(step_a, n_j, 2 * hw) for r2 in range(rows)], axis=1
        ).astype(BF16)
        scores = lax.dot_general(
            queries, keys, (((2,), (2,)), ((0,), (0,))), preferred_element_type=F32
        ) + bias[None]
        weights = jnp.exp(scores - jnp.max(scores, axis=-1, keepdims=True))
        total = jnp.sum(weights, axis=-1, keepdims=True)
        mixed = lax.dot_general(
            weights.astype(BF16), keys, (((2,), (1,)), ((0,), (0,))), preferred_element_type=F32
        ) / total
        attended = mixed[:, :n_j]
        for t in range(1, n_h):
            attended = jnp.where(
                (lane >= hw + t * HD)[None], mixed[:, t * n_j : (t + 1) * n_j], attended
            )
        gated = jnp.where(
            (lane >= hw)[None], attended.astype(BF16).astype(F32) * qg3, 0.0
        )
        gown[at, :] = gated.reshape(flat_a, 2 * hw).astype(BF16)
        for d in range(1, heads):
            gated_copy(step, d, at).start()

    def project(step):
        at = pl.ds(pl.multiple_of(step * flat_a, 16), flat_a)
        acc = dot(gown[at, :], out_weights[0])
        for d in range(1, heads):
            gated_copy(step, d, at).wait()
            acc += dot(goth[d, at, :], out_weights[d])
        out[at, :] = acc.astype(out.dtype)

    if steps <= 4:
        for step in range(steps):
            attend(step)
        for step in range(steps):
            project(step)
    else:
        pl.loop(0, steps)(attend)
        pl.loop(0, steps)(project)

    for p in range(pieces_sent):
        for c2 in range(cols):
            target, slot, copy = bias_copy(p, c2)

            @pl.when(jnp.logical_or(target != r, c != c2))
            def _():
                copy.wait_send()


def per_device(
    mesh_sizes, pair_rep, pad_mask, chain_breaks, w_query, w_key, w_value, w_gate, w_bias,
    chain_bias, w_out
):
    rows, cols, heads = mesh_sizes
    n_i, n_j, channels = pair_rep.shape
    n_h = chain_bias.shape[0]
    hw = n_h * HD
    n_k = rows * n_j
    total = n_i * n_j
    piece = min(n_i, n_j)
    lanes_k = -(-n_k // 128) * 128
    step_a = largest_divisor(n_i, max(2, 40 * 1024 // (n_h * n_j * lanes_k)), 2)
    steps = n_i // step_a
    share = w_out.shape[1] // heads
    hbm = pl.BlockSpec(memory_space=pltpu.HBM)
    vmem = pl.BlockSpec(memory_space=pltpu.VMEM)
    dma = pltpu.SemaphoreType.DMA
    scratch = [
        pltpu.VMEM((rows, total, channels), BF16),
        pltpu.VMEM((2, 2 * hw, channels), BF16),
        pltpu.VMEM((n_h, channels), BF16),
        pltpu.VMEM((heads, hw, w_out.shape[1]), BF16),
        pltpu.VMEM((1, n_k), jnp.int32),
        pltpu.SMEM(chain_breaks.shape, jnp.int32),
        pltpu.SMEM(chain_bias.shape, F32),
        pltpu.VMEM((total, 2 * hw), F32),
        pltpu.VMEM((rows, total, 2 * hw), F32),
        pltpu.VMEM((n_i // piece, n_h, piece, n_j), F32),
        pltpu.VMEM((rows, n_j // piece, n_h, piece, n_j), F32),
        pltpu.VMEM((n_h, n_j, n_k), F32),
        pltpu.VMEM((total, 2 * hw), BF16),
        pltpu.VMEM((heads, total, 2 * hw), BF16),
        dma((10,)),
        dma((rows,)),
        dma((rows,)),
        dma((heads,)),
        dma((heads,)),
        dma((n_i // piece, cols)),
        dma((rows, n_j // piece)),
        dma((heads, steps)),
        dma((heads, steps)),
    ]
    update = pl.pallas_call(
        functools.partial(kernel, (rows, cols, heads, n_i, n_j, n_h, channels)),
        out_shape=jax.ShapeDtypeStruct((total, share), BF16),
        in_specs=[hbm] * 10,
        out_specs=vmem,
        scratch_shapes=scratch,
        compiler_params=pltpu.CompilerParams(
            collective_id=0,
            has_side_effects=True,
            vmem_limit_bytes=60 << 20,
        ),
    )(
        pair_rep.reshape(total, channels), pad_mask.reshape(1, n_k), chain_breaks, chain_bias,
        w_query.T, w_key.T, w_value.T, w_gate.T, w_bias.T, w_out,
    )
    return update.reshape(n_i, n_j, share)


def solution(mesh):
    placed = (
        P(("groups", "col"), "row", None),
        P("groups"),
        P("groups"),
        P(None, "head"),
        P(None, "head"),
        P(None, "head"),
        P(None, "head"),
        P(None, "head"),
        P("head"),
        P("head", None),
    )
    sizes = (mesh.shape["row"], mesh.shape["col"], mesh.shape["head"])
    return jax.shard_map(
        functools.partial(per_device, sizes),
        mesh=mesh,
        in_specs=placed,
        out_specs=P(("groups", "col"), "row", "head"),
        check_vma=False,
    )
```

```python
import functools

import jax
import jax.numpy as jnp
from jax import lax
from jax.experimental import pallas as pl
from jax.experimental.pallas import tpu as pltpu
from jax.sharding import PartitionSpec as P

HD = 32
MESH = pl.DeviceIdType.MESH
F32 = jnp.float32
BF16 = jnp.bfloat16
NT = (((1,), (1,)), ((), ()))


def layer_norm(x):
    centred = x - jnp.mean(x, axis=-1, keepdims=True)
    spread = jnp.mean(centred * centred, axis=-1, keepdims=True)
    return centred * lax.rsqrt(spread + 1e-05)


def dot(a, b):
    return jnp.dot(a, b, preferred_element_type=F32)


def dot_t(a, b):
    return lax.dot_general(a, b, NT, preferred_element_type=F32)


def largest_divisor(n, limit, step=1):
    best = step
    for d in range(step, n + 1, step):
        if n % d == 0 and d <= limit:
            best = d
    return best


def kernel(
    sizes,
    pair, mask, breaks, chain_bias, wq, wk, wv, wg, wb, wo,
    gout, owout,
    xs, wbuf, wbbuf, wobuf, maskbuf, breakbuf, cbbuf, qg, kv, bsend, brecv, bfull, gown, owbuf,
    local_sem, x_send, x_recv, wo_send, wo_recv, b_send, b_recv, g_send, g_recv, own_sem,
):
    rows, cols, heads, n_i, n_j, n_h, channels = sizes
    n_k = rows * n_j
    hw = n_h * HD
    piece = bsend.shape[2]
    r, c, h = lax.axis_index("row"), lax.axis_index("col"), lax.axis_index("head")

    barrier = pltpu.get_barrier_semaphore()
    for r2 in range(rows):
        for c2 in range(cols):
            @pl.when(jnp.logical_or(r != r2, c != c2))
            def _():
                pl.semaphore_signal(
                    barrier, inc=1, device_id={"row": r2, "col": c2}, device_id_type=MESH
                )
    for d in range(1, heads):
        pl.semaphore_signal(
            barrier, inc=1, device_id={"head": lax.rem(h + d, heads)}, device_id_type=MESH
        )

    locals_ = [
        pltpu.make_async_copy(pair, xs.at[r], local_sem.at[0]),
        pltpu.make_async_copy(wb, wbbuf, local_sem.at[1]),
        pltpu.make_async_copy(wq, wbuf.at[0, pl.ds(0, hw)], local_sem.at[2]),
        pltpu.make_async_copy(wg, wbuf.at[0, pl.ds(hw, hw)], local_sem.at[3]),
        pltpu.make_async_copy(wk, wbuf.at[1, pl.ds(0, hw)], local_sem.at[4]),
        pltpu.make_async_copy(wv, wbuf.at[1, pl.ds(hw, hw)], local_sem.at[5]),
        pltpu.make_async_copy(wo, wobuf.at[0], local_sem.at[6]),
        pltpu.make_async_copy(mask, maskbuf, local_sem.at[7]),
        pltpu.make_async_copy(breaks, breakbuf, local_sem.at[8]),
        pltpu.make_async_copy(chain_bias, cbbuf, local_sem.at[9]),
    ]
    for copy in locals_:
        copy.start()

    pl.semaphore_wait(barrier, rows * cols - 1 + heads - 1)

    x_copies = []
    for d in range(1, rows):
        copy = pltpu.make_async_remote_copy(
            src_ref=pair, dst_ref=xs.at[r], send_sem=x_send.at[d], recv_sem=x_recv.at[d],
            device_id={"row": lax.rem(r + d, rows)}, device_id_type=MESH,
        )
        copy.start()
        x_copies.append(copy)
    wo_copies = []
    for d in range(1, heads):
        copy = pltpu.make_async_remote_copy(
            src_ref=wo, dst_ref=wobuf.at[d], send_sem=wo_send.at[d], recv_sem=wo_recv.at[d],
            device_id={"head": lax.rem(h + d, heads)}, device_id_type=MESH,
        )
        copy.start()
        wo_copies.append(copy)

    for copy in locals_:
        copy.wait()

    wqg, wkv = wbuf[0], wbuf[1]
    wbt = jnp.concatenate(
        [wbbuf[...].astype(F32), jnp.zeros((16 - n_h, channels), F32)], axis=0
    ).astype(BF16)

    lane = lax.broadcasted_iota(jnp.int32, (1, 2 * hw), 1)
    step_i = largest_divisor(n_i, 12, 2)
    flat = step_i * n_j
    own_normed = []
    for first in range(0, n_i, step_i):
        normed = layer_norm(xs[r, pl.ds(first * n_j, flat), :].astype(F32))
        normed3 = normed.reshape(step_i, n_j, channels).astype(BF16)
        for i in range(step_i):
            line = lax.dot_general(wbt, normed3[i], NT, preferred_element_type=F32)
            p, at = divmod(first + i, piece)
            for head in range(n_h):
                bsend[p, head, pl.ds(at, 1), :] = line[head : head + 1]
        own_normed.append(normed.astype(BF16))

    def bias_copy(p, c2):
        start = c * n_i + p * piece
        target = start // n_j
        slot = (start - target * n_j) // piece
        return target, slot, pltpu.make_async_remote_copy(
            src_ref=bsend.at[p], dst_ref=brecv.at[r, slot],
            send_sem=b_send.at[p, c2], recv_sem=b_recv.at[r, slot],
            device_id={"row": target, "col": c2}, device_id_type=MESH,
        )

    pieces_sent = n_i // piece
    for p in range(pieces_sent):
        for c2 in range(cols):
            target, slot, copy = bias_copy(p, c2)
            here = jnp.logical_and(target == r, c == c2)

            @pl.when(jnp.logical_not(here))
            def _():
                copy.start()

            @pl.when(here)
            def _():
                brecv[r, slot] = bsend[p]

    for step, first in enumerate(range(0, n_i, step_i)):
        at = pl.ds(first * n_j, flat)
        both = dot_t(own_normed[step], wqg)
        qg[at, :] = jnp.where(
            lane < hw, (both * HD ** (-0.5)).astype(BF16).astype(F32),
            jax.nn.sigmoid(both).astype(BF16).astype(F32),
        )
        kv[r, at, :] = dot_t(own_normed[step], wkv)

    key_pos = lax.broadcasted_iota(jnp.int32, (n_j, n_k), 1)
    query_pos = r * n_j + lax.broadcasted_iota(jnp.int32, (n_j, n_k), 0)
    key_chain = jnp.zeros((n_j, n_k), jnp.int32)
    query_chain = jnp.zeros((n_j, n_k), jnp.int32)
    for b in range(breaks.shape[0]):
        key_chain += (breakbuf[b] <= key_pos).astype(jnp.int32)
        query_chain += (breakbuf[b] <= query_pos).astype(jnp.int32)
    across = (key_chain != query_chain).astype(F32)
    mask_term = (maskbuf[...].astype(F32) - 1.0) * 1000000000.0

    own_rows = wobuf.shape[1]
    share = wobuf.shape[2] // heads

    def out_weight(d):
        full = wobuf[d].astype(F32)
        mine = full[:, :share]
        for t in range(1, heads):
            mine = jnp.where(h == t, full[:, t * share : (t + 1) * share], mine)
        return jnp.concatenate([jnp.zeros((hw, share), F32), mine], axis=0).astype(BF16)

    for copy in wo_copies:
        copy.wait()
    for d in range(heads):
        owbuf[d] = out_weight(d)
    weight_out = pltpu.make_async_copy(owbuf, owout, local_sem.at[10])
    weight_out.start()

    for d in range(1, rows):
        x_copies[d - 1].wait()
        source = lax.rem(r + rows - d, rows)
        for first in range(0, n_i, step_i):
            at = pl.ds(first * n_j, flat)
            normed = layer_norm(xs[source, at, :].astype(F32)).astype(BF16)
            kv[source, at, :] = dot_t(normed, wkv)

    slots = n_j // piece
    for slot in range(slots):
        source_c = (r * n_j + slot * piece) // n_i
        for r2 in range(rows):
            @pl.when(jnp.logical_or(r2 != r, source_c != c))
            def _():
                pltpu.make_async_remote_copy(
                    src_ref=bsend.at[0], dst_ref=brecv.at[r2, slot],
                    send_sem=b_send.at[0, 0], recv_sem=b_recv.at[r2, slot],
                    device_id={"row": r2}, device_id_type=MESH,
                ).wait_recv()
    for slot in range(slots):
        for r2 in range(rows):
            for head in range(n_h):
                bfull[head, pl.ds(slot * piece, piece), pl.ds(r2 * n_j, n_j)] = brecv[
                    r2, slot, head
                ]
    bias = jnp.concatenate(
        [bfull[head] + (cbbuf[head] * across + mask_term) for head in range(n_h)], axis=0
    )

    lanes_k = -(-n_k // 128) * 128
    step_a = largest_divisor(n_i, max(2, 40 * 1024 // (n_h * n_j * lanes_k)), 2)
    flat_a = step_a * n_j
    steps = n_i // step_a

    def gated_copy(step, d, at):
        return pltpu.make_async_remote_copy(
            src_ref=gown.at[at, :], dst_ref=gout.at[d, at, :],
            send_sem=g_send.at[d, step], recv_sem=g_recv.at[d, step],
            device_id={"head": lax.rem(h + d, heads)}, device_id_type=MESH,
        )

    def own_copy(step, at):
        return pltpu.make_async_copy(gown.at[at, :], gout.at[0, at, :], own_sem.at[step])

    def attend(step):
        at = pl.ds(pl.multiple_of(step * flat_a, 16), flat_a)
        qg3 = qg[at, :].reshape(step_a, n_j, 2 * hw)
        queries = jnp.concatenate(
            [
                jnp.where(jnp.logical_and(lane >= t * HD, lane < (t + 1) * HD)[None], qg3, 0.0)
                for t in range(n_h)
            ],
            axis=1,
        ).astype(BF16)
        keys = jnp.concatenate(
            [kv[r2, at, :].reshape(step_a, n_j, 2 * hw) for r2 in range(rows)], axis=1
        ).astype(BF16)
        scores = lax.dot_general(
            queries, keys, (((2,), (2,)), ((0,), (0,))), preferred_element_type=F32
        ) + bias[None]
        weights = jnp.exp(scores - jnp.max(scores, axis=-1, keepdims=True))
        total = jnp.sum(weights, axis=-1, keepdims=True)
        mixed = lax.dot_general(
            weights.astype(BF16), keys, (((2,), (1,)), ((0,), (0,))), preferred_element_type=F32
        ) / total
        attended = mixed[:, :n_j]
        for t in range(1, n_h):
            attended = jnp.where(
                (lane >= hw + t * HD)[None], mixed[:, t * n_j : (t + 1) * n_j], attended
            )
        gated = jnp.where(
            (lane >= hw)[None], attended.astype(BF16).astype(F32) * qg3, 0.0
        )
        gown[at, :] = gated.reshape(flat_a, 2 * hw).astype(BF16)
        for d in range(1, heads):
            gated_copy(step, d, at).start()
        own_copy(step, at).start()

    def finish(step):
        at = pl.ds(pl.multiple_of(step * flat_a, 16), flat_a)
        own_copy(step, at).wait()
        for d in range(1, heads):
            gated_copy(step, d, at).wait()

    if steps <= 4:
        for step in range(steps):
            attend(step)
        for step in range(steps):
            finish(step)
    else:
        pl.loop(0, steps)(attend)
        pl.loop(0, steps)(finish)
    weight_out.wait()

    for p in range(pieces_sent):
        for c2 in range(cols):
            target, slot, copy = bias_copy(p, c2)

            @pl.when(jnp.logical_or(target != r, c != c2))
            def _():
                copy.wait_send()


def project(gated, weights, out):
    acc = dot(gated[0], weights[0])
    for d in range(1, gated.shape[0]):
        acc += dot(gated[d], weights[d])
    out[...] = acc.astype(out.dtype)


def per_device(
    mesh_sizes, pair_rep, pad_mask, chain_breaks, w_query, w_key, w_value, w_gate, w_bias,
    chain_bias, w_out
):
    rows, cols, heads = mesh_sizes
    n_i, n_j, channels = pair_rep.shape
    n_h = chain_bias.shape[0]
    hw = n_h * HD
    n_k = rows * n_j
    total = n_i * n_j
    piece = min(n_i, n_j)
    lanes_k = -(-n_k // 128) * 128
    step_a = largest_divisor(n_i, max(2, 40 * 1024 // (n_h * n_j * lanes_k)), 2)
    steps = n_i // step_a
    share = w_out.shape[1] // heads
    hbm = pl.BlockSpec(memory_space=pltpu.HBM)
    vmem = pl.BlockSpec(memory_space=pltpu.VMEM)
    dma = pltpu.SemaphoreType.DMA
    scratch = [
        pltpu.VMEM((rows, total, channels), BF16),
        pltpu.VMEM((2, 2 * hw, channels), BF16),
        pltpu.VMEM((n_h, channels), BF16),
        pltpu.VMEM((heads, hw, w_out.shape[1]), BF16),
        pltpu.VMEM((1, n_k), jnp.int32),
        pltpu.SMEM(chain_breaks.shape, jnp.int32),
        pltpu.SMEM(chain_bias.shape, F32),
        pltpu.VMEM((total, 2 * hw), F32),
        pltpu.VMEM((rows, total, 2 * hw), F32),
        pltpu.VMEM((n_i // piece, n_h, piece, n_j), F32),
        pltpu.VMEM((rows, n_j // piece, n_h, piece, n_j), F32),
        pltpu.VMEM((n_h, n_j, n_k), F32),
        pltpu.VMEM((total, 2 * hw), BF16),
        pltpu.VMEM((heads, 2 * hw, share), BF16),
        dma((11,)),
        dma((rows,)),
        dma((rows,)),
        dma((heads,)),
        dma((heads,)),
        dma((n_i // piece, cols)),
        dma((rows, n_j // piece)),
        dma((heads, steps)),
        dma((heads, steps)),
        dma((steps,)),
    ]
    gated, weights = pl.pallas_call(
        functools.partial(kernel, (rows, cols, heads, n_i, n_j, n_h, channels)),
        out_shape=[
            jax.ShapeDtypeStruct((heads, total, 2 * hw), BF16),
            jax.ShapeDtypeStruct((heads, 2 * hw, share), BF16),
        ],
        in_specs=[hbm] * 10,
        out_specs=[hbm, hbm],
        scratch_shapes=scratch,
        compiler_params=pltpu.CompilerParams(
            collective_id=0,
            has_side_effects=True,
            vmem_limit_bytes=60 << 20,
        ),
    )(
        pair_rep.reshape(total, channels), pad_mask.reshape(1, n_k), chain_breaks, chain_bias,
        w_query.T, w_key.T, w_value.T, w_gate.T, w_bias.T, w_out,
    )
    update = pl.pallas_call(
        project,
        out_shape=jax.ShapeDtypeStruct((total, share), BF16),
        in_specs=[vmem, vmem],
        out_specs=vmem,
        compiler_params=pltpu.CompilerParams(vmem_limit_bytes=60 << 20),
    )(gated, weights)
    return update.reshape(n_i, n_j, share)


def solution(mesh):
    placed = (
        P(("groups", "col"), "row", None),
        P("groups"),
        P("groups"),
        P(None, "head"),
        P(None, "head"),
        P(None, "head"),
        P(None, "head"),
        P(None, "head"),
        P("head"),
        P("head", None),
    )
    sizes = (mesh.shape["row"], mesh.shape["col"], mesh.shape["head"])
    return jax.shard_map(
        functools.partial(per_device, sizes),
        mesh=mesh,
        in_specs=placed,
        out_specs=P(("groups", "col"), "row", "head"),
        check_vma=False,
    )
```

```python
import functools

import jax
import jax.numpy as jnp
from jax import lax
from jax.experimental import pallas as pl
from jax.experimental.pallas import tpu as pltpu
from jax.sharding import PartitionSpec as P

HD = 32
MESH = pl.DeviceIdType.MESH
F32 = jnp.float32
BF16 = jnp.bfloat16
NT = (((1,), (1,)), ((), ()))


def layer_norm(x):
    centred = x - jnp.mean(x, axis=-1, keepdims=True)
    spread = jnp.mean(centred * centred, axis=-1, keepdims=True)
    return centred * lax.rsqrt(spread + 1e-05)


def dot(a, b):
    return jnp.dot(a, b, preferred_element_type=F32)


def dot_t(a, b):
    return lax.dot_general(a, b, NT, preferred_element_type=F32)


def largest_divisor(n, limit, step=1):
    best = step
    for d in range(step, n + 1, step):
        if n % d == 0 and d <= limit:
            best = d
    return best


def kernel(
    sizes,
    pair, mask, breaks, chain_bias, wq, wk, wv, wg, wb, wo,
    gout, owout,
    xs, wbuf, wbbuf, wobuf, maskbuf, breakbuf, cbbuf, qg, kv, bsend, brecv, bfull, gown, owbuf,
    local_sem, x_send, x_recv, wo_send, wo_recv, b_send, b_recv, g_send, g_recv, own_sem,
):
    rows, cols, heads, n_i, n_j, n_h, channels = sizes
    n_k = rows * n_j
    hw = n_h * HD
    piece = bsend.shape[2]
    r, c, h = lax.axis_index("row"), lax.axis_index("col"), lax.axis_index("head")

    barrier = pltpu.get_barrier_semaphore()
    for d in range(1, rows):
        pl.semaphore_signal(
            barrier, inc=1, device_id={"row": lax.rem(r + d, rows)}, device_id_type=MESH
        )
    for slot in range(n_j // piece):
        source_c = (r * n_j + slot * piece) // n_i
        for r2 in range(rows):
            @pl.when(jnp.logical_or(r2 != r, source_c != c))
            def _():
                pl.semaphore_signal(
                    barrier, inc=1, device_id={"row": r2, "col": source_c}, device_id_type=MESH
                )
    for d in range(1, heads):
        pl.semaphore_signal(
            barrier, inc=1, device_id={"head": lax.rem(h + d, heads)}, device_id_type=MESH
        )

    locals_ = [
        pltpu.make_async_copy(pair, xs.at[r], local_sem.at[0]),
        pltpu.make_async_copy(wb, wbbuf, local_sem.at[1]),
        pltpu.make_async_copy(wq, wbuf.at[0, pl.ds(0, hw)], local_sem.at[2]),
        pltpu.make_async_copy(wg, wbuf.at[0, pl.ds(hw, hw)], local_sem.at[3]),
        pltpu.make_async_copy(wk, wbuf.at[1, pl.ds(0, hw)], local_sem.at[4]),
        pltpu.make_async_copy(wv, wbuf.at[1, pl.ds(hw, hw)], local_sem.at[5]),
        pltpu.make_async_copy(wo, wobuf.at[0], local_sem.at[6]),
        pltpu.make_async_copy(mask, maskbuf, local_sem.at[7]),
        pltpu.make_async_copy(breaks, breakbuf, local_sem.at[8]),
        pltpu.make_async_copy(chain_bias, cbbuf, local_sem.at[9]),
    ]
    for copy in locals_:
        copy.start()

    copies_out = rows - 1 + heads - 1
    for p in range(n_i // piece):
        here = ((c * n_i + p * piece) // n_j == r).astype(jnp.int32)
        copies_out = copies_out + cols - here
    pl.semaphore_wait(barrier, copies_out)

    x_copies = []
    for d in range(1, rows):
        copy = pltpu.make_async_remote_copy(
            src_ref=pair, dst_ref=xs.at[r], send_sem=x_send.at[d], recv_sem=x_recv.at[d],
            device_id={"row": lax.rem(r + d, rows)}, device_id_type=MESH,
        )
        copy.start()
        x_copies.append(copy)
    wo_copies = []
    for d in range(1, heads):
        copy = pltpu.make_async_remote_copy(
            src_ref=wo, dst_ref=wobuf.at[d], send_sem=wo_send.at[d], recv_sem=wo_recv.at[d],
            device_id={"head": lax.rem(h + d, heads)}, device_id_type=MESH,
        )
        copy.start()
        wo_copies.append(copy)

    for copy in locals_:
        copy.wait()

    wqg, wkv = wbuf[0], wbuf[1]
    wbt = jnp.concatenate(
        [wbbuf[...].astype(F32), jnp.zeros((16 - n_h, channels), F32)], axis=0
    ).astype(BF16)

    lane = lax.broadcasted_iota(jnp.int32, (1, 2 * hw), 1)
    step_i = largest_divisor(n_i, 12, 2)
    flat = step_i * n_j
    own_normed = []
    for first in range(0, n_i, step_i):
        normed = layer_norm(xs[r, pl.ds(first * n_j, flat), :].astype(F32))
        normed3 = normed.reshape(step_i, n_j, channels).astype(BF16)
        for i in range(step_i):
            line = lax.dot_general(wbt, normed3[i], NT, preferred_element_type=F32)
            p, at = divmod(first + i, piece)
            for head in range(n_h):
                bsend[p, head, pl.ds(at, 1), :] = line[head : head + 1]
        own_normed.append(normed.astype(BF16))

    def bias_copy(p, c2):
        start = c * n_i + p * piece
        target = start // n_j
        slot = (start - target * n_j) // piece
        return target, slot, pltpu.make_async_remote_copy(
            src_ref=bsend.at[p], dst_ref=brecv.at[r, slot],
            send_sem=b_send.at[p, c2], recv_sem=b_recv.at[r, slot],
            device_id={"row": target, "col": c2}, device_id_type=MESH,
        )

    pieces_sent = n_i // piece
    for p in range(pieces_sent):
        for c2 in range(cols):
            target, slot, copy = bias_copy(p, c2)
            here = jnp.logical_and(target == r, c == c2)

            @pl.when(jnp.logical_not(here))
            def _():
                copy.start()

            @pl.when(here)
            def _():
                brecv[r, slot] = bsend[p]

    for step, first in enumerate(range(0, n_i, step_i)):
        at = pl.ds(first * n_j, flat)
        both = dot_t(own_normed[step], wqg)
        qg[at, :] = jnp.where(
            lane < hw, (both * HD ** (-0.5)).astype(BF16).astype(F32),
            jax.nn.sigmoid(both).astype(BF16).astype(F32),
        )
        kv[r, at, :] = dot_t(own_normed[step], wkv)

    key_pos = lax.broadcasted_iota(jnp.int32, (n_j, n_k), 1)
    query_pos = r * n_j + lax.broadcasted_iota(jnp.int32, (n_j, n_k), 0)
    key_chain = jnp.zeros((n_j, n_k), jnp.int32)
    query_chain = jnp.zeros((n_j, n_k), jnp.int32)
    for b in range(breaks.shape[0]):
        key_chain += (breakbuf[b] <= key_pos).astype(jnp.int32)
        query_chain += (breakbuf[b] <= query_pos).astype(jnp.int32)
    across = (key_chain != query_chain).astype(F32)
    mask_term = (maskbuf[...].astype(F32) - 1.0) * 1000000000.0

    own_rows = wobuf.shape[1]
    share = wobuf.shape[2] // heads

    def out_weight(d):
        full = wobuf[d].astype(F32)
        mine = full[:, :share]
        for t in range(1, heads):
            mine = jnp.where(h == t, full[:, t * share : (t + 1) * share], mine)
        return jnp.concatenate([jnp.zeros((hw, share), F32), mine], axis=0).astype(BF16)

    for copy in wo_copies:
        copy.wait()
    for d in range(heads):
        owbuf[d] = out_weight(d)
    weight_out = pltpu.make_async_copy(owbuf, owout, local_sem.at[10])
    weight_out.start()

    for d in range(1, rows):
        x_copies[d - 1].wait()
        source = lax.rem(r + rows - d, rows)
        for first in range(0, n_i, step_i):
            at = pl.ds(first * n_j, flat)
            normed = layer_norm(xs[source, at, :].astype(F32)).astype(BF16)
            kv[source, at, :] = dot_t(normed, wkv)

    slots = n_j // piece
    for slot in range(slots):
        source_c = (r * n_j + slot * piece) // n_i
        for r2 in range(rows):
            @pl.when(jnp.logical_or(r2 != r, source_c != c))
            def _():
                pltpu.make_async_remote_copy(
                    src_ref=bsend.at[0], dst_ref=brecv.at[r2, slot],
                    send_sem=b_send.at[0, 0], recv_sem=b_recv.at[r2, slot],
                    device_id={"row": r2}, device_id_type=MESH,
                ).wait_recv()
    for slot in range(slots):
        for r2 in range(rows):
            for head in range(n_h):
                bfull[head, pl.ds(slot * piece, piece), pl.ds(r2 * n_j, n_j)] = brecv[
                    r2, slot, head
                ]
    bias = jnp.concatenate(
        [bfull[head] + (cbbuf[head] * across + mask_term) for head in range(n_h)], axis=0
    )

    lanes_k = -(-n_k // 128) * 128
    step_a = largest_divisor(n_i, max(2, 40 * 1024 // (n_h * n_j * lanes_k)), 2)
    flat_a = step_a * n_j
    steps = n_i // step_a

    def gated_copy(step, d, at):
        return pltpu.make_async_remote_copy(
            src_ref=gown.at[at, :], dst_ref=gout.at[d, at, :],
            send_sem=g_send.at[d, step], recv_sem=g_recv.at[d, step],
            device_id={"head": lax.rem(h + d, heads)}, device_id_type=MESH,
        )

    def own_copy(step, at):
        return pltpu.make_async_copy(gown.at[at, :], gout.at[0, at, :], own_sem.at[step])

    def attend(step):
        at = pl.ds(pl.multiple_of(step * flat_a, 16), flat_a)
        qg3 = qg[at, :].reshape(step_a, n_j, 2 * hw)
        queries = jnp.concatenate(
            [
                jnp.where(jnp.logical_and(lane >= t * HD, lane < (t + 1) * HD)[None], qg3, 0.0)
                for t in range(n_h)
            ],
            axis=1,
        ).astype(BF16)
        keys = jnp.concatenate(
            [kv[r2, at, :].reshape(step_a, n_j, 2 * hw) for r2 in range(rows)], axis=1
        ).astype(BF16)
        scores = lax.dot_general(
            queries, keys, (((2,), (2,)), ((0,), (0,))), preferred_element_type=F32
        ) + bias[None]
        weights = jnp.exp(scores - jnp.max(scores, axis=-1, keepdims=True))
        total = jnp.sum(weights, axis=-1, keepdims=True)
        mixed = lax.dot_general(
            weights.astype(BF16), keys, (((2,), (1,)), ((0,), (0,))), preferred_element_type=F32
        ) / total
        attended = mixed[:, :n_j]
        for t in range(1, n_h):
            attended = jnp.where(
                (lane >= hw + t * HD)[None], mixed[:, t * n_j : (t + 1) * n_j], attended
            )
        gated = jnp.where(
            (lane >= hw)[None], attended.astype(BF16).astype(F32) * qg3, 0.0
        )
        gown[at, :] = gated.reshape(flat_a, 2 * hw).astype(BF16)
        for d in range(1, heads):
            gated_copy(step, d, at).start()
        own_copy(step, at).start()

    def finish(step):
        at = pl.ds(pl.multiple_of(step * flat_a, 16), flat_a)
        own_copy(step, at).wait()
        for d in range(1, heads):
            gated_copy(step, d, at).wait()

    if steps <= 4:
        for step in range(steps):
            attend(step)
        for step in range(steps):
            finish(step)
    else:
        pl.loop(0, steps)(attend)
        pl.loop(0, steps)(finish)
    weight_out.wait()

    for p in range(pieces_sent):
        for c2 in range(cols):
            target, slot, copy = bias_copy(p, c2)

            @pl.when(jnp.logical_or(target != r, c != c2))
            def _():
                copy.wait_send()


def project(gated, weights, out):
    acc = dot(gated[0], weights[0])
    for d in range(1, gated.shape[0]):
        acc += dot(gated[d], weights[d])
    out[...] = acc.astype(out.dtype)


def per_device(
    mesh_sizes, pair_rep, pad_mask, chain_breaks, w_query, w_key, w_value, w_gate, w_bias,
    chain_bias, w_out
):
    rows, cols, heads = mesh_sizes
    n_i, n_j, channels = pair_rep.shape
    n_h = chain_bias.shape[0]
    hw = n_h * HD
    n_k = rows * n_j
    total = n_i * n_j
    piece = min(n_i, n_j)
    lanes_k = -(-n_k // 128) * 128
    step_a = largest_divisor(n_i, max(2, 40 * 1024 // (n_h * n_j * lanes_k)), 2)
    steps = n_i // step_a
    share = w_out.shape[1] // heads
    hbm = pl.BlockSpec(memory_space=pltpu.HBM)
    vmem = pl.BlockSpec(memory_space=pltpu.VMEM)
    dma = pltpu.SemaphoreType.DMA
    scratch = [
        pltpu.VMEM((rows, total, channels), BF16),
        pltpu.VMEM((2, 2 * hw, channels), BF16),
        pltpu.VMEM((n_h, channels), BF16),
        pltpu.VMEM((heads, hw, w_out.shape[1]), BF16),
        pltpu.VMEM((1, n_k), jnp.int32),
        pltpu.SMEM(chain_breaks.shape, jnp.int32),
        pltpu.SMEM(chain_bias.shape, F32),
        pltpu.VMEM((total, 2 * hw), F32),
        pltpu.VMEM((rows, total, 2 * hw), F32),
        pltpu.VMEM((n_i // piece, n_h, piece, n_j), F32),
        pltpu.VMEM((rows, n_j // piece, n_h, piece, n_j), F32),
        pltpu.VMEM((n_h, n_j, n_k), F32),
        pltpu.VMEM((total, 2 * hw), BF16),
        pltpu.VMEM((heads, 2 * hw, share), BF16),
        dma((11,)),
        dma((rows,)),
        dma((rows,)),
        dma((heads,)),
        dma((heads,)),
        dma((n_i // piece, cols)),
        dma((rows, n_j // piece)),
        dma((heads, steps)),
        dma((heads, steps)),
        dma((steps,)),
    ]
    gated, weights = pl.pallas_call(
        functools.partial(kernel, (rows, cols, heads, n_i, n_j, n_h, channels)),
        out_shape=[
            jax.ShapeDtypeStruct((heads, total, 2 * hw), BF16),
            jax.ShapeDtypeStruct((heads, 2 * hw, share), BF16),
        ],
        in_specs=[hbm] * 10,
        out_specs=[hbm, hbm],
        scratch_shapes=scratch,
        compiler_params=pltpu.CompilerParams(
            collective_id=0,
            has_side_effects=True,
            vmem_limit_bytes=60 << 20,
        ),
    )(
        pair_rep.reshape(total, channels), pad_mask.reshape(1, n_k), chain_breaks, chain_bias,
        w_query.T, w_key.T, w_value.T, w_gate.T, w_bias.T, w_out,
    )
    update = pl.pallas_call(
        project,
        out_shape=jax.ShapeDtypeStruct((total, share), BF16),
        in_specs=[vmem, vmem],
        out_specs=vmem,
        compiler_params=pltpu.CompilerParams(vmem_limit_bytes=60 << 20),
    )(gated, weights)
    return update.reshape(n_i, n_j, share)


def solution(mesh):
    placed = (
        P(("groups", "col"), "row", None),
        P("groups"),
        P("groups"),
        P(None, "head"),
        P(None, "head"),
        P(None, "head"),
        P(None, "head"),
        P(None, "head"),
        P("head"),
        P("head", None),
    )
    sizes = (mesh.shape["row"], mesh.shape["col"], mesh.shape["head"])
    return jax.shard_map(
        functools.partial(per_device, sizes),
        mesh=mesh,
        in_specs=placed,
        out_specs=P(("groups", "col"), "row", "head"),
        check_vma=False,
    )
```

```python
import functools

import jax
import jax.numpy as jnp
from jax import lax
from jax.experimental import pallas as pl
from jax.experimental.pallas import tpu as pltpu
from jax.sharding import PartitionSpec as P

HD = 32
MESH = pl.DeviceIdType.MESH
F32 = jnp.float32
BF16 = jnp.bfloat16
NT = (((1,), (1,)), ((), ()))


def layer_norm(x):
    centred = x - jnp.mean(x, axis=-1, keepdims=True)
    spread = jnp.mean(centred * centred, axis=-1, keepdims=True)
    return centred * lax.rsqrt(spread + 1e-05)


def dot(a, b):
    return jnp.dot(a, b, preferred_element_type=F32)


def dot_t(a, b):
    return lax.dot_general(a, b, NT, preferred_element_type=F32)


def largest_divisor(n, limit, step=1):
    best = step
    for d in range(step, n + 1, step):
        if n % d == 0 and d <= limit:
            best = d
    return best


def kernel(
    sizes,
    pair, mask, breaks, chain_bias, wq, wk, wv, wg, wb, wo,
    gout, owout,
    xs, wbuf, wbbuf, wobuf, maskbuf, breakbuf, cbbuf, qg, kv, bsend, brecv, bfull, gown, owbuf,
    local_sem, x_send, x_recv, wo_send, wo_recv, b_send, b_recv, g_send, g_recv, own_sem,
):
    rows, cols, heads, n_i, n_j, n_h, channels = sizes
    n_k = rows * n_j
    hw = n_h * HD
    piece = bsend.shape[2]
    r, c, h = lax.axis_index("row"), lax.axis_index("col"), lax.axis_index("head")

    barrier = pltpu.get_barrier_semaphore()
    for d in range(1, rows):
        pl.semaphore_signal(
            barrier, inc=1, device_id={"row": lax.rem(r + d, rows)}, device_id_type=MESH
        )
    for slot in range(n_j // piece):
        source_c = (r * n_j + slot * piece) // n_i
        for r2 in range(rows):
            @pl.when(jnp.logical_or(r2 != r, source_c != c))
            def _():
                pl.semaphore_signal(
                    barrier, inc=1, device_id={"row": r2, "col": source_c}, device_id_type=MESH
                )
    for d in range(1, heads):
        pl.semaphore_signal(
            barrier, inc=1, device_id={"head": lax.rem(h + d, heads)}, device_id_type=MESH
        )

    locals_ = [
        pltpu.make_async_copy(pair, xs.at[r], local_sem.at[0]),
        pltpu.make_async_copy(wb, wbbuf, local_sem.at[1]),
        pltpu.make_async_copy(wq, wbuf.at[0, pl.ds(0, hw)], local_sem.at[2]),
        pltpu.make_async_copy(wg, wbuf.at[0, pl.ds(hw, hw)], local_sem.at[3]),
        pltpu.make_async_copy(wk, wbuf.at[1, pl.ds(0, hw)], local_sem.at[4]),
        pltpu.make_async_copy(wv, wbuf.at[1, pl.ds(hw, hw)], local_sem.at[5]),
        pltpu.make_async_copy(wo, wobuf.at[0], local_sem.at[6]),
        pltpu.make_async_copy(mask, maskbuf, local_sem.at[7]),
        pltpu.make_async_copy(breaks, breakbuf, local_sem.at[8]),
        pltpu.make_async_copy(chain_bias, cbbuf, local_sem.at[9]),
    ]
    for copy in locals_:
        copy.start()

    for copy in locals_:
        copy.wait()

    wqg, wkv = wbuf[0], wbuf[1]
    wbt = jnp.concatenate(
        [wbbuf[...].astype(F32), jnp.zeros((16 - n_h, channels), F32)], axis=0
    ).astype(BF16)

    lane = lax.broadcasted_iota(jnp.int32, (1, 2 * hw), 1)
    step_i = largest_divisor(n_i, 12, 2)
    flat = step_i * n_j
    own_normed = []
    for first in range(0, n_i, step_i):
        normed = layer_norm(xs[r, pl.ds(first * n_j, flat), :].astype(F32))
        normed3 = normed.reshape(step_i, n_j, channels).astype(BF16)
        for i in range(step_i):
            line = lax.dot_general(wbt, normed3[i], NT, preferred_element_type=F32)
            p, at = divmod(first + i, piece)
            for head in range(n_h):
                bsend[p, head, pl.ds(at, 1), :] = line[head : head + 1]
        own_normed.append(normed.astype(BF16))

    for step, first in enumerate(range(0, n_i, step_i)):
        at = pl.ds(first * n_j, flat)
        both = dot_t(own_normed[step], wqg)
        qg[at, :] = jnp.where(
            lane < hw, (both * HD ** (-0.5)).astype(BF16).astype(F32),
            jax.nn.sigmoid(both).astype(BF16).astype(F32),
        )
        kv[r, at, :] = dot_t(own_normed[step], wkv)

    key_pos = lax.broadcasted_iota(jnp.int32, (n_j, n_k), 1)
    query_pos = r * n_j + lax.broadcasted_iota(jnp.int32, (n_j, n_k), 0)
    key_chain = jnp.zeros((n_j, n_k), jnp.int32)
    query_chain = jnp.zeros((n_j, n_k), jnp.int32)
    for b in range(breaks.shape[0]):
        key_chain += (breakbuf[b] <= key_pos).astype(jnp.int32)
        query_chain += (breakbuf[b] <= query_pos).astype(jnp.int32)
    across = (key_chain != query_chain).astype(F32)
    mask_term = (maskbuf[...].astype(F32) - 1.0) * 1000000000.0

    copies_out = rows - 1 + heads - 1
    for p in range(n_i // piece):
        here = ((c * n_i + p * piece) // n_j == r).astype(jnp.int32)
        copies_out = copies_out + cols - here
    pl.semaphore_wait(barrier, copies_out)

    x_parts = 2 if n_i % 2 == 0 and (n_i // 2 * n_j) % 16 == 0 else 1
    part_i = n_i // x_parts

    def x_copy(d, part):
        at = pl.ds(part * part_i * n_j, part_i * n_j)
        return pltpu.make_async_remote_copy(
            src_ref=pair.at[at, :], dst_ref=xs.at[r, at, :],
            send_sem=x_send.at[d, part], recv_sem=x_recv.at[d, part],
            device_id={"row": lax.rem(r + d, rows)}, device_id_type=MESH,
        )

    for d in range(1, rows):
        x_copy(d, 0).start()
    def bias_copy(p, c2):
        start = c * n_i + p * piece
        target = start // n_j
        slot = (start - target * n_j) // piece
        return target, slot, pltpu.make_async_remote_copy(
            src_ref=bsend.at[p], dst_ref=brecv.at[r, slot],
            send_sem=b_send.at[p, c2], recv_sem=b_recv.at[r, slot],
            device_id={"row": target, "col": c2}, device_id_type=MESH,
        )

    pieces_sent = n_i // piece
    for p in range(pieces_sent):
        for c2 in range(cols):
            target, slot, copy = bias_copy(p, c2)
            here = jnp.logical_and(target == r, c == c2)

            @pl.when(jnp.logical_not(here))
            def _():
                copy.start()

            @pl.when(here)
            def _():
                brecv[r, slot] = bsend[p]

    for part in range(1, x_parts):
        for d in range(1, rows):
            x_copy(d, part).start()
    wo_copies = []
    for d in range(1, heads):
        copy = pltpu.make_async_remote_copy(
            src_ref=wo, dst_ref=wobuf.at[d], send_sem=wo_send.at[d], recv_sem=wo_recv.at[d],
            device_id={"head": lax.rem(h + d, heads)}, device_id_type=MESH,
        )
        copy.start()
        wo_copies.append(copy)

    own_rows = wobuf.shape[1]
    share = wobuf.shape[2] // heads

    def out_weight(d):
        full = wobuf[d].astype(F32)
        mine = full[:, :share]
        for t in range(1, heads):
            mine = jnp.where(h == t, full[:, t * share : (t + 1) * share], mine)
        return jnp.concatenate([jnp.zeros((hw, share), F32), mine], axis=0).astype(BF16)

    for copy in wo_copies:
        copy.wait()
    for d in range(heads):
        owbuf[d] = out_weight(d)
    weight_out = pltpu.make_async_copy(owbuf, owout, local_sem.at[10])
    weight_out.start()

    def take(part):
        step_x = largest_divisor(part_i, 12, 2)
        for d in range(1, rows):
            x_copy(d, part).wait()
            source = lax.rem(r + rows - d, rows)
            for first in range(part * part_i, (part + 1) * part_i, step_x):
                at = pl.ds(first * n_j, step_x * n_j)
                normed = layer_norm(xs[source, at, :].astype(F32)).astype(BF16)
                kv[source, at, :] = dot_t(normed, wkv)

    take(0)

    slots = n_j // piece
    for slot in range(slots):
        source_c = (r * n_j + slot * piece) // n_i
        for r2 in range(rows):
            @pl.when(jnp.logical_or(r2 != r, source_c != c))
            def _():
                pltpu.make_async_remote_copy(
                    src_ref=bsend.at[0], dst_ref=brecv.at[r2, slot],
                    send_sem=b_send.at[0, 0], recv_sem=b_recv.at[r2, slot],
                    device_id={"row": r2}, device_id_type=MESH,
                ).wait_recv()
    for slot in range(slots):
        for r2 in range(rows):
            for head in range(n_h):
                bfull[head, pl.ds(slot * piece, piece), pl.ds(r2 * n_j, n_j)] = brecv[
                    r2, slot, head
                ]
    bias = jnp.concatenate(
        [bfull[head] + (cbbuf[head] * across + mask_term) for head in range(n_h)], axis=0
    )

    lanes_k = -(-n_k // 128) * 128
    step_a = largest_divisor(n_i // 2, max(2, 40 * 1024 // (n_h * n_j * lanes_k)), 2)
    flat_a = step_a * n_j
    steps = n_i // step_a

    def gated_copy(step, d, at):
        return pltpu.make_async_remote_copy(
            src_ref=gown.at[at, :], dst_ref=gout.at[d, at, :],
            send_sem=g_send.at[d, step], recv_sem=g_recv.at[d, step],
            device_id={"head": lax.rem(h + d, heads)}, device_id_type=MESH,
        )

    def own_copy(step, at):
        return pltpu.make_async_copy(gown.at[at, :], gout.at[0, at, :], own_sem.at[step])

    def attend(step):
        at = pl.ds(pl.multiple_of(step * flat_a, 16), flat_a)
        qg3 = qg[at, :].reshape(step_a, n_j, 2 * hw)
        queries = jnp.concatenate(
            [
                jnp.where(jnp.logical_and(lane >= t * HD, lane < (t + 1) * HD)[None], qg3, 0.0)
                for t in range(n_h)
            ],
            axis=1,
        ).astype(BF16)
        keys = jnp.concatenate(
            [kv[r2, at, :].reshape(step_a, n_j, 2 * hw) for r2 in range(rows)], axis=1
        ).astype(BF16)
        scores = lax.dot_general(
            queries, keys, (((2,), (2,)), ((0,), (0,))), preferred_element_type=F32
        ) + bias[None]
        weights = jnp.exp(scores - jnp.max(scores, axis=-1, keepdims=True))
        total = jnp.sum(weights, axis=-1, keepdims=True)
        mixed = lax.dot_general(
            weights.astype(BF16), keys, (((2,), (1,)), ((0,), (0,))), preferred_element_type=F32
        ) / total
        attended = mixed[:, :n_j]
        for t in range(1, n_h):
            attended = jnp.where(
                (lane >= hw + t * HD)[None], mixed[:, t * n_j : (t + 1) * n_j], attended
            )
        gated = jnp.where(
            (lane >= hw)[None], attended.astype(BF16).astype(F32) * qg3, 0.0
        )
        gown[at, :] = gated.reshape(flat_a, 2 * hw).astype(BF16)
        for d in range(1, heads):
            gated_copy(step, d, at).start()
        own_copy(step, at).start()

    def finish(step):
        at = pl.ds(pl.multiple_of(step * flat_a, 16), flat_a)
        own_copy(step, at).wait()
        for d in range(1, heads):
            gated_copy(step, d, at).wait()

    for part in range(x_parts):
        if part > 0:
            take(part)
        low, high = part * part_i // step_a, (part + 1) * part_i // step_a
        if steps <= 4:
            for step in range(low, high):
                attend(step)
        else:
            pl.loop(low, high)(attend)
    if steps <= 4:
        for step in range(steps):
            finish(step)
    else:
        pl.loop(0, steps)(finish)
    weight_out.wait()

    for p in range(pieces_sent):
        for c2 in range(cols):
            target, slot, copy = bias_copy(p, c2)

            @pl.when(jnp.logical_or(target != r, c != c2))
            def _():
                copy.wait_send()


def project(gated, weights, out):
    acc = dot(gated[0], weights[0])
    for d in range(1, gated.shape[0]):
        acc += dot(gated[d], weights[d])
    out[...] = acc.astype(out.dtype)


def per_device(
    mesh_sizes, pair_rep, pad_mask, chain_breaks, w_query, w_key, w_value, w_gate, w_bias,
    chain_bias, w_out
):
    rows, cols, heads = mesh_sizes
    n_i, n_j, channels = pair_rep.shape
    n_h = chain_bias.shape[0]
    hw = n_h * HD
    n_k = rows * n_j
    total = n_i * n_j
    piece = min(n_i, n_j)
    lanes_k = -(-n_k // 128) * 128
    step_a = largest_divisor(n_i // 2, max(2, 40 * 1024 // (n_h * n_j * lanes_k)), 2)
    steps = n_i // step_a
    share = w_out.shape[1] // heads
    hbm = pl.BlockSpec(memory_space=pltpu.HBM)
    vmem = pl.BlockSpec(memory_space=pltpu.VMEM)
    dma = pltpu.SemaphoreType.DMA
    scratch = [
        pltpu.VMEM((rows, total, channels), BF16),
        pltpu.VMEM((2, 2 * hw, channels), BF16),
        pltpu.VMEM((n_h, channels), BF16),
        pltpu.VMEM((heads, hw, w_out.shape[1]), BF16),
        pltpu.VMEM((1, n_k), jnp.int32),
        pltpu.SMEM(chain_breaks.shape, jnp.int32),
        pltpu.SMEM(chain_bias.shape, F32),
        pltpu.VMEM((total, 2 * hw), F32),
        pltpu.VMEM((rows, total, 2 * hw), F32),
        pltpu.VMEM((n_i // piece, n_h, piece, n_j), F32),
        pltpu.VMEM((rows, n_j // piece, n_h, piece, n_j), F32),
        pltpu.VMEM((n_h, n_j, n_k), F32),
        pltpu.VMEM((total, 2 * hw), BF16),
        pltpu.VMEM((heads, 2 * hw, share), BF16),
        dma((11,)),
        dma((rows, 2)),
        dma((rows, 2)),
        dma((heads,)),
        dma((heads,)),
        dma((n_i // piece, cols)),
        dma((rows, n_j // piece)),
        dma((heads, steps)),
        dma((heads, steps)),
        dma((steps,)),
    ]
    gated, weights = pl.pallas_call(
        functools.partial(kernel, (rows, cols, heads, n_i, n_j, n_h, channels)),
        out_shape=[
            jax.ShapeDtypeStruct((heads, total, 2 * hw), BF16),
            jax.ShapeDtypeStruct((heads, 2 * hw, share), BF16),
        ],
        in_specs=[hbm] * 10,
        out_specs=[hbm, hbm],
        scratch_shapes=scratch,
        compiler_params=pltpu.CompilerParams(
            collective_id=0,
            has_side_effects=True,
            vmem_limit_bytes=60 << 20,
        ),
    )(
        pair_rep.reshape(total, channels), pad_mask.reshape(1, n_k), chain_breaks, chain_bias,
        w_query.T, w_key.T, w_value.T, w_gate.T, w_bias.T, w_out,
    )
    update = pl.pallas_call(
        project,
        out_shape=jax.ShapeDtypeStruct((total, share), BF16),
        in_specs=[vmem, vmem],
        out_specs=vmem,
        compiler_params=pltpu.CompilerParams(vmem_limit_bytes=60 << 20),
    )(gated, weights)
    return update.reshape(n_i, n_j, share)


def solution(mesh):
    placed = (
        P(("groups", "col"), "row", None),
        P("groups"),
        P("groups"),
        P(None, "head"),
        P(None, "head"),
        P(None, "head"),
        P(None, "head"),
        P(None, "head"),
        P("head"),
        P("head", None),
    )
    sizes = (mesh.shape["row"], mesh.shape["col"], mesh.shape["head"])
    return jax.shard_map(
        functools.partial(per_device, sizes),
        mesh=mesh,
        in_specs=placed,
        out_specs=P(("groups", "col"), "row", "head"),
        check_vma=False,
    )
```
